32 devices in a mesh: member: 2 (over y), lon: 4 (over x, core), lat: 4 (over z).
Axes of the slice: x: 2, y: 2, z: 4, core: 2. Of those that a mesh axis runs over, the one named last changes fastest.
Arguments:
- heat_content: float32 [32, 256, 512], P(None, ('member', 'lat'), 'lon'), parts along dimension 1, may hold values from -6 to 6
- sea_height: float32 [256, 512], P(('member', 'lat'), 'lon'), parts along dimension 0, may hold values from -6 to 6
- closing_heat_sensitivity: float32 [32, 256, 512], P(None, ('member', 'lat'), 'lon'), parts along dimension 1, may hold values from -6 to 6
- closing_height_sensitivity: float32 [256, 512], P(('member', 'lat'), 'lon'), parts along dimension 0, may hold values from -6 to 6
- mixing_coefficient: float32 [128, 512], P('lat', 'lon'), may hold values from 0.02 to 0.2
- sea_indicator: int32 [128, 512], P('lat', 'lon'), may hold values 0 or 1
- water_layer_count: int32 [128, 512], P('lat', 'lon'), may hold values from 1 to 32
Outputs:
- temperature_grad: float32 [32, 256, 512], P(None, ('member', 'lat'), 'lon'), parts along dimension 1
- surface_grad: float32 [256, 512], P(('member', 'lat'), 'lon'), parts along dimension 0
- diffusivity_grad: float32 [256, 512], P(('member', 'lat'), 'lon'), parts along dimension 0
The draws below stay inside these ranges and needn't reach their ends.
There are 2 independent parts, one for each index of `member`. The reference program is written for one: setup_inputs(seed, part) draws one part's arguments, and reference() takes and returns one part's arrays. A program takes and returns all parts, laid end to end along the dimension named above; an argument that names none is the same for every part. Nothing has to cross between parts.
All inputs are finite; a program needn't handle non-finite values. No bound on the sum of `sea_indicator` on one device may be relied on, other than what follows from the above.
Results may differ from the reference program's by a relative error of at most 0.0001.
Values sent between devices are 32-bit elements; how exact they have to be, the bound alone decides.
A program may use at most 64 MiB of HBM per device.

```python
import math
import jax
import jax.numpy as jnp
from jax import lax

LAYER_COUNT = 32
ITERS = 4
EAST_WEST_LINES = 512
NORTH_SOUTH_LINES = 128


def plant(drawn, stream_key, least, high):
    index_at = [jax.random.randint(jax.random.fold_in(stream_key, axis), (), 0, length) for axis, length in enumerate(drawn.shape)]
    longest = drawn.shape.index(max(drawn.shape))
    next_to = index_at[:longest] + [(index_at[longest] + 1) % drawn.shape[longest]] + index_at[longest + 1:]
    return drawn.at[tuple(index_at)].set(least).at[tuple(next_to)].set(high)


def block_scale(own_key, dims, cuts, smallest, largest):
    def one(position, shards_of):
        steps = jax.random.uniform(jax.random.fold_in(jax.random.fold_in(own_key, 6), position), (shards_of,), jnp.float32, smallest / len(cuts), largest / len(cuts))
        return jnp.repeat(jnp.exp(steps), dims[position] // shards_of).reshape((-1,) + (1,) * (len(dims) - position - 1))

    gain = one(*cuts[0])
    for cut in cuts[1:]:
        gain = gain * one(*cut)
    return gain


def gaussian(key, extent, width, bound, cuts=(), kind=jnp.bfloat16):
    entries = jax.random.normal(key, extent, jnp.float32) * width
    if len(cuts) > 0:
        entries = block_scale(key, extent, cuts, -0.22, 0.18) * entries
    return jnp.clip(entries, min=-bound, max=bound).astype(kind)


def setup_inputs(seed: int = 0, part: int = 0) -> dict:
    splits = jax.random.split(jax.random.key(seed), 8)
    part_keys = jax.random.split(jax.random.fold_in(splits[7], part), 8)
    heat_content = gaussian(part_keys[0], (LAYER_COUNT, NORTH_SOUTH_LINES, EAST_WEST_LINES), 1.0, 6.0, ((1, 4), (2, 4)), jnp.float32)
    sea_height = gaussian(part_keys[1], (NORTH_SOUTH_LINES, EAST_WEST_LINES), 1.0, 6.0, ((0, 4), (1, 4)), jnp.float32)
    closing_heat_sensitivity = gaussian(part_keys[2], (LAYER_COUNT, NORTH_SOUTH_LINES, EAST_WEST_LINES), 1.0, 6.0, ((1, 4), (2, 4)), jnp.float32)
    closing_height_sensitivity = gaussian(part_keys[3], (NORTH_SOUTH_LINES, EAST_WEST_LINES), 1.0, 6.0, ((0, 4), (1, 4)), jnp.float32)
    mixing_coefficient = jnp.clip(jnp.exp(math.log(0.2) - 2.3025851 * jax.random.uniform(splits[4], (NORTH_SOUTH_LINES, EAST_WEST_LINES), jnp.float32) ** block_scale(splits[4], (NORTH_SOUTH_LINES, EAST_WEST_LINES), ((0, 4), (1, 4)), -0.2, 0.2)), 0.02, 0.2)
    sea_indicator = plant((jax.random.randint(splits[5], (NORTH_SOUTH_LINES, EAST_WEST_LINES), 0, 10) < 9).astype(jnp.int32), jax.random.fold_in(splits[5], 1), 0, 1)
    water_layer_count = plant(jax.random.randint(splits[6], (NORTH_SOUTH_LINES, EAST_WEST_LINES), 1, LAYER_COUNT + 1), jax.random.fold_in(splits[6], 1), 1, LAYER_COUNT).astype(jnp.int32)
    return dict(heat_content=heat_content, sea_height=sea_height, closing_heat_sensitivity=closing_heat_sensitivity, closing_height_sensitivity=closing_height_sensitivity, mixing_coefficient=mixing_coefficient, sea_indicator=sea_indicator, water_layer_count=water_layer_count)


EOS_QUAD = 0.1
PRESS_COEF = 0.5
SURF_COEF = 4.0
COUPLING = 1.0

def northward(field):
    return jnp.concatenate([field[..., 1:, :], jnp.zeros_like(field[..., :1, :])], axis=-2)

def eastward(field):
    return jnp.roll(field, -1, axis=-1)

def southward(flux):
    return jnp.concatenate([jnp.zeros_like(flux[..., :1, :]), flux[..., :-1, :]], axis=-2)

def laplace(field, weight_x, weight_y):
    flux_x = weight_x * (eastward(field) - field)
    flux_y = weight_y * (northward(field) - field)
    return flux_x - jnp.roll(flux_x, 1, axis=-1) + flux_y - southward(flux_y)

def level_axis():
    return jnp.arange(LAYER_COUNT, dtype=jnp.float32)[:, None, None]

def evaluate_hydrostatic_load(state, water_site_indicator):
    heights = (level_axis() + 0.5) / LAYER_COUNT
    return lax.optimization_barrier(jnp.sum(water_site_indicator * heights * (state + EOS_QUAD * state * state), axis=0)) / math.sqrt(LAYER_COUNT)

def poisson_inversion(rhs, eastward_thickness, northward_thickness):
    solution = jnp.zeros_like(rhs)
    residual = rhs
    direction = rhs
    norm_now = jnp.sum(residual * residual)
    for iteration in range(ITERS):
        image = direction - SURF_COEF * laplace(direction, eastward_thickness, northward_thickness)
        step_size = norm_now / jnp.sum(direction * image)
        solution = solution + step_size * direction
        residual = residual - step_size * image
        norm_next = jnp.sum(residual * residual)
        direction = residual + norm_next / norm_now * direction
        norm_now = norm_next
    return solution

def reference(heat_content, sea_height, closing_heat_sensitivity, closing_height_sensitivity, mixing_coefficient, sea_indicator, water_layer_count):
    land_f = sea_indicator.astype(jnp.float32)
    water_site_indicator = land_f[None] * (level_axis() < water_layer_count.astype(jnp.float32)[None]).astype(jnp.float32)
    depth_col = lax.optimization_barrier(jnp.sum(water_site_indicator, axis=0)) / LAYER_COUNT
    land_x = land_f * eastward(land_f)
    land_y = land_f * northward(land_f)
    eastward_thickness = jnp.minimum(depth_col, eastward(depth_col)) * land_x
    northward_thickness = jnp.minimum(depth_col, northward(depth_col)) * land_y
    profile = 1.0 - level_axis() / LAYER_COUNT

    def scalar_concentration(state, surface_new, diff):
        kappa_x = 0.5 * (diff + eastward(diff)) * water_site_indicator * eastward(water_site_indicator)
        kappa_y = 0.5 * (diff + northward(diff)) * water_site_indicator * northward(water_site_indicator)
        diffused = state + laplace(state, kappa_x, kappa_y)
        return water_site_indicator * (diffused + COUPLING * profile * surface_new[None])

    def sea_height_rim(state, surf):
        return surf - PRESS_COEF * laplace(evaluate_hydrostatic_load(state, water_site_indicator), land_x, land_y)
    trailing_piece = scalar_concentration(heat_content, poisson_inversion(sea_height_rim(heat_content, sea_height), eastward_thickness, northward_thickness), mixing_coefficient)

    def reverse_sweep_once(state, back_temp, back_surf):
        unused, pull_tracer = jax.vjp(scalar_concentration, state, jnp.zeros_like(sea_height), mixing_coefficient)
        temp_part, surf_part, grad_kappa = pull_tracer(back_temp)
        back_rhs = poisson_inversion(back_surf + surf_part, eastward_thickness, northward_thickness)
        unused_too, pull_surface = jax.vjp(sea_height_rim, state, sea_height)
        temp_extra, surf_extra = pull_surface(back_rhs)
        return (temp_part + temp_extra, surf_extra, grad_kappa)
    heat_content_later, sea_height_later, sensitivity_later_moment = reverse_sweep_once(trailing_piece, closing_heat_sensitivity, closing_height_sensitivity)
    heat_content_earlier, sea_height_earlier, sensitivity_earlier_moment = reverse_sweep_once(heat_content, heat_content_later, sea_height_later)
    return (heat_content_earlier, sea_height_earlier, sensitivity_later_moment + sensitivity_earlier_moment)
```

```python
import functools
import math

import jax
import jax.numpy as jnp
from jax import lax
from jax.experimental import pallas as pl
from jax.experimental.pallas import tpu as pltpu
from jax.sharding import PartitionSpec as P

EOS_QUAD = 0.1
PRESS_COEF = 0.5
SURF_COEF = 4.0
COUPLING = 1.0

MESH = pl.DeviceIdType.MESH
RIM = 8
STEP = 4
SHIFT = 1.2
LINK = 0.2
ENTRIES = 11
WAYS = ((1, 0), (-1, 0), (0, 1), (0, -1), (1, 1), (-1, 1), (1, -1), (-1, -1))
BACK = tuple(WAYS.index((-a, -b)) for a, b in WAYS)


def rolled(x, shift, axis):
    return pltpu.roll(x, shift % x.shape[axis], axis)


def kernel(
    heat_hbm, height, closing_hbm, closing_height, mixing, sea, layers,
    out_ref, surface_ref, diff_ref,
    heat_v, closing_v, m0_v, t1_v, u_v, m1_v, w2,
    mine_a, ew_a, d_a, mine_b, ew_b, d_b, mine_c, ew_c, d_c,
    pack_1, rp_1, row_1n, row_1s, rr_1, pack_2, rp_2, row_2n, row_2s, rr_2,
    vec_0, slots_0, vec_1, slots_1, vec_2, slots_2,
    load_sem, send_h, recv_h, send_p, recv_p, send_g, recv_g,
):
    levels, rows, lanes = heat_v.shape
    n_lon, n_lat = lax.axis_size("lon"), lax.axis_size("lat")
    group = n_lon * n_lat
    lon, lat = lax.axis_index("lon"), lax.axis_index("lat")
    me = lat * n_lon + lon

    heat_load = pltpu.make_async_copy(heat_hbm, heat_v, load_sem.at[0])
    closing_load = pltpu.make_async_copy(closing_hbm, closing_v, load_sem.at[1])
    heat_load.start()
    closing_load.start()

    def peer(index):
        return {"lon": lax.rem(index, n_lon), "lat": lax.div(index, n_lon)}

    barrier = pltpu.get_barrier_semaphore()

    def greet(step, carry):
        pl.semaphore_signal(
            barrier, inc=1, device_id=peer(lax.rem(me + step, group)), device_id_type=MESH
        )
        return carry

    lax.fori_loop(1, group, greet, 0)

    def there(way):
        if WAYS[way][1] == 1:
            return lat < n_lat - 1
        if WAYS[way][1] == -1:
            return lat > 0
        return None

    def when(cond, action):
        if cond is None:
            action()
        else:
            pl.when(cond)(action)

    def target(way):
        return {
            "lon": lax.rem(lon + WAYS[way][0] + n_lon, n_lon),
            "lat": lat + WAYS[way][1],
        }

    def clear_south():
        for ref in (d_a, d_b, d_c):
            for slot in (1, 4, 5):
                ref[slot] = jnp.zeros(ref.shape[1:], jnp.float32)
        for ref in (rr_1, rr_2):
            ref[1] = jnp.zeros(ref.shape[1:], jnp.float32)

    def clear_north():
        for ref in (d_a, d_b, d_c):
            for slot in (0, 2, 3):
                ref[slot] = jnp.zeros(ref.shape[1:], jnp.float32)
        for ref in (rr_1, rr_2):
            ref[0] = jnp.zeros(ref.shape[1:], jnp.float32)

    pl.when(lat == 0)(clear_south)
    pl.when(lat == n_lat - 1)(clear_north)

    def halo(mine, ew, d, turn):
        copies = []
        for way in range(8):
            slot = BACK[way]
            if way < 2:
                src, dst = mine, ew.at[slot]
            else:
                first = rows - RIM if WAYS[way][1] == 1 else 0
                src, dst = mine.at[:, pl.ds(first, RIM), :], d.at[slot - 2]
            copies.append(
                pltpu.make_async_remote_copy(
                    src_ref=src,
                    dst_ref=dst,
                    send_sem=send_h.at[turn * 8 + way],
                    recv_sem=recv_h.at[turn * 8 + slot],
                    device_id=target(way),
                    device_id_type=MESH,
                )
            )
        return copies

    def columns(pack, rp, row_n, row_s, rr, turn):
        copies = []
        for way in range(4):
            slot = BACK[way]
            src = (pack, pack, row_n, row_s)[way]
            dst = rp.at[slot] if way < 2 else rr.at[slot - 2]
            copies.append(
                pltpu.make_async_remote_copy(
                    src_ref=src,
                    dst_ref=dst,
                    send_sem=send_p.at[turn * 4 + way],
                    recv_sem=recv_p.at[turn * 4 + slot],
                    device_id=target(way),
                    device_id_type=MESH,
                )
            )
        return copies

    def start(copies):
        for way, copy in enumerate(copies):
            when(there(way), copy.start)

    def arrive(copies):
        for way, copy in enumerate(copies):
            when(there(BACK[way]), copy.wait_recv)

    def sent(copies):
        for way, copy in enumerate(copies):
            when(there(way), copy.wait_send)

    def share(vec, slots, turn):
        def one(step, carry):
            pltpu.make_async_remote_copy(
                src_ref=vec,
                dst_ref=slots.at[me],
                send_sem=send_g.at[turn],
                recv_sem=recv_g.at[turn],
                device_id=peer(lax.rem(me + step, group)),
                device_id_type=MESH,
            ).start()
            return carry

        slots[me] = vec[...]
        lax.fori_loop(1, group, one, 0)

    def shared(slots, sem, turn):
        several = slots.at[pl.ds(0, group - 1)]
        pltpu.make_async_copy(several, several, sem.at[turn]).wait()

    halo_a = halo(mine_a, ew_a, d_a, 0)
    halo_b = halo(mine_b, ew_b, d_b, 1)
    halo_c = halo(mine_c, ew_c, d_c, 2)
    cols_1 = columns(pack_1, rp_1, row_1n, row_1s, rr_1, 0)
    cols_2 = columns(pack_2, rp_2, row_2n, row_2s, rr_2, 1)

    lane = lax.broadcasted_iota(jnp.int32, (rows, lanes), 1)
    row = lax.broadcasted_iota(jnp.int32, (rows, lanes), 0)
    lane_8 = lax.broadcasted_iota(jnp.int32, (8, lanes), 1)
    sub_8 = lax.broadcasted_iota(jnp.int32, (8, lanes), 0)

    code = (sea[...] * layers[...]).astype(jnp.float32)
    mine_a[0] = code
    mine_a[1] = mixing[...]
    mine_a[2] = height[...]

    def folded(x):
        total = x[0:8]
        for i in range(8, x.shape[0], 8):
            total = total + x[i : i + 8]
        return jnp.sum(total, axis=0, keepdims=True)

    def gathered(sums, places):
        result = jnp.zeros((1, lanes), jnp.float32)
        for first in range(0, len(sums), 8):
            some = sums[first : first + 8]
            table = jnp.zeros((8, lanes), jnp.float32)
            spot = jnp.full((8, lanes), -1, jnp.int32)
            for i, item in enumerate(some):
                table = jnp.where(sub_8 == i, item, table)
                spot = jnp.where(sub_8 == i, places[first + i], spot)
            column = jnp.sum(table, axis=1, keepdims=True)
            result = result + jnp.sum(
                jnp.where(lane_8 == spot, column, 0.0), axis=0, keepdims=True
            )
        return result

    share_of = code * (SURF_COEF / levels)
    east = jnp.minimum(share_of, rolled(share_of, -1, 1))
    north = jnp.minimum(share_of, rolled(share_of, -1, 0))
    diagonal = east + rolled(east, 1, 1) + north + rolled(north, 1, 0)
    second_moment = diagonal * diagonal + 2.0 * (east * east + north * north)
    vec_0[...] = gathered([folded(diagonal), folded(second_moment)], [0, 1])

    pl.semaphore_wait(barrier, group - 1)
    start(halo_a)
    share(vec_0, slots_0, 0)

    heat_load.wait()
    closing_load.wait()

    def level_of(k):
        return k.astype(jnp.float32)

    def load_body(block, carry):
        press, total = carry
        for i in range(STEP):
            k = block * STEP + i
            kf = level_of(k)
            h = heat_v[k]
            wet = code > kf
            masked = jnp.where(wet, closing_v[k], 0.0)
            m0_v[k] = masked
            press = press + jnp.where(
                wet, (kf + 0.5) / levels * (h + EOS_QUAD * h * h), 0.0
            )
            total = total + COUPLING * (1.0 - kf / levels) * masked
        return press, total

    zero = jnp.zeros((rows, lanes), jnp.float32)
    press, total_one = lax.fori_loop(
        0, levels // STEP, load_body, (zero, closing_height[...])
    )
    mine_b[0] = press / math.sqrt(levels)
    mine_b[1] = total_one
    start(halo_b)

    def packing(first_v, second_v, pack, row_n, row_s):
        def body(block, packed):
            for i in range(STEP):
                k = block * STEP + i
                a = first_v[k]
                b = second_v[k]
                packed = jnp.where((lane >> 1) == k, pltpu.roll(a, 2 * k + 1, 1), packed)
                packed = jnp.where(
                    (lane >> 1) == k + levels,
                    pltpu.roll(b, 2 * k + 2 * levels + 1, 1),
                    packed,
                )
                row_n[pl.ds(k, 1), :] = a[rows - 1 : rows, :]
                row_n[pl.ds(k + levels, 1), :] = b[rows - 1 : rows, :]
                row_s[pl.ds(k, 1), :] = a[0:1, :]
                row_s[pl.ds(k + levels, 1), :] = b[0:1, :]
            return packed

        pack[...] = lax.fori_loop(0, levels // STEP, body, zero)

    packing(heat_v, m0_v, pack_1, row_1n, row_1s)
    start(cols_1)

    def wide(mine, ew, d, f):
        half = lax.broadcasted_iota(jnp.int32, (rows, lanes), 1) < lanes // 2
        half_8 = lax.broadcasted_iota(jnp.int32, (RIM, lanes), 1) < lanes // 2
        left = jnp.concatenate([mine[f], d[0, f], d[1, f]], axis=0)
        right = jnp.concatenate(
            [
                jnp.where(half, ew[0, f], ew[1, f]),
                jnp.where(half_8, d[2, f], d[3, f]),
                jnp.where(half_8, d[4, f], d[5, f]),
            ],
            axis=0,
        )
        return jnp.concatenate([left, right], axis=1)

    def own(x):
        return x[:rows, :lanes]

    def sides(x):
        return rolled(x, -1, 1), rolled(x, 1, 1), rolled(x, -1, 0), rolled(x, 1, 0)

    arrive(halo_a)
    code_w = wide(mine_a, ew_a, d_a, 0)
    mix_w = wide(mine_a, ew_a, d_a, 1)
    height_w = wide(mine_a, ew_a, d_a, 2)
    near_code = [jnp.minimum(code_w, x) for x in sides(code_w)]
    for i, x in enumerate(near_code):
        w2[i] = own(x)
    for i, x in enumerate(sides(mix_w)):
        w2[4 + i] = own(0.5 * (mix_w + x))
    face_land = [jnp.where(x > 0.0, 1.0, 0.0) for x in near_code]
    for i, x in enumerate(face_land):
        w2[8 + i] = own(x) * PRESS_COEF

    def totals(slots):
        return jnp.broadcast_to(jnp.sum(slots[...], axis=0), (8, lanes))

    def at(total, entry):
        return pltpu.roll(total, (lanes - entry) % lanes, 1)

    def scalar(x):
        return x[0:1, 0:1]

    shared(slots_0, recv_g, 0)
    moments = totals(slots_0)
    trace = at(moments, 0)
    ratio = jnp.where(trace > 0.0, at(moments, 1) / jnp.where(trace > 0.0, trace, 1.0), 1.0)
    scale = jnp.where(lane_8 < lanes // 2, ratio, pltpu.roll(ratio, lanes // 2, 1))
    weight = scalar(1.0 / scale) * (SURF_COEF / levels)
    solver_w = [x * weight for x in near_code]

    def apply(v):
        around = sides(v)
        result = solver_w[0] * (v - around[0])
        for w, x in zip(solver_w[1:], around[1:]):
            result = result + w * (v - x)
        return result

    def basis(b):
        v1 = apply(b)
        v2 = apply(v1) - SHIFT * v1
        v3 = apply(v2) - SHIFT * v2 - LINK * v1
        v4 = own(apply(v3))
        o = [own(v) for v in (b, v1, v2, v3)]
        pairs = ((0, 0), (0, 1), (0, 2), (0, 3), (1, 1), (1, 2), (1, 3), (2, 2), (2, 3), (3, 3))
        sums = [folded(o[i] * o[j]) for i, j in pairs] + [folded(o[3] * v4)]
        return (b, v1, v2, v3), sums

    def coefficients(total):
        g00, g01, g02, g03, g11, g12, g13, g22, g23, g33, g34 = [
            at(total, e) for e in range(ENTRIES)
        ]
        m = {
            (0, 0): g00 + scale * g01,
            (0, 1): g01 + scale * g11,
            (0, 2): g02 + scale * g12,
            (0, 3): g03 + scale * g13,
            (1, 1): g11 + scale * (g12 + SHIFT * g11),
            (1, 2): g12 + scale * (g22 + SHIFT * g12),
            (1, 3): g13 + scale * (g23 + SHIFT * g13),
            (2, 2): g22 + scale * (g23 + SHIFT * g22 + LINK * g12),
            (2, 3): g23 + scale * (g33 + SHIFT * g23 + LINK * g13),
            (3, 3): g33 + scale * g34,
        }
        c = [g00, g01, g02, g03]
        low, inverse = {}, []
        work = dict(m)
        for j in range(4):
            pivot = work[j, j]
            good = pivot > 3e-7 * m[j, j]
            inv = jnp.where(good, 1.0 / jnp.where(good, pivot, 1.0), 0.0)
            inverse.append(inv)
            for i in range(j + 1, 4):
                low[i, j] = work[j, i] * inv
            for i in range(j + 1, 4):
                for k in range(i, 4):
                    work[i, k] = work[i, k] - low[i, j] * work[j, k]
                c[i] = c[i] - low[i, j] * c[j]
        c = [x * inv for x, inv in zip(c, inverse)]
        for i in (2, 1, 0):
            for j in range(i + 1, 4):
                c[i] = c[i] - low[j, i] * c[j]
        return c

    def combined(c, vs):
        result = scalar(c[0]) * vs[0]
        for a, v in zip(c[1:], vs[1:]):
            result = result + scalar(a) * v
        return result

    def pressed(x):
        around = sides(x)
        centre = own(x)
        result = w2[8] * (centre - own(around[0]))
        for i in range(1, 4):
            result = result + w2[8 + i] * (centre - own(around[i]))
        return result * (1.0 / math.sqrt(levels))

    arrive(halo_b)
    press_w = wide(mine_b, ew_b, d_b, 0)
    rhs = height_w
    for w, x in zip(face_land, sides(press_w)):
        rhs = rhs + (PRESS_COEF * w) * (press_w - x)
    basis_1, sums_1 = basis(rhs)
    basis_2, sums_2 = basis(wide(mine_b, ew_b, d_b, 1))
    half = lanes // 2
    vec_1[...] = gathered(
        sums_1 + sums_2, list(range(ENTRIES)) + [half + e for e in range(ENTRIES)]
    )
    share(vec_1, slots_1, 1)

    def mixed(rp):
        return jnp.where((lane & 1) == 0, rolled(rp[0], -1, 1), rolled(rp[1], 1, 1))

    def around_of(v, rim, shift, rr, k):
        r = pltpu.roll(rim, shift, 1)
        return (
            jnp.where(lane == lanes - 1, r, rolled(v, -1, 1)),
            jnp.where(lane == 0, r, rolled(v, 1, 1)),
            jnp.where(row == rows - 1, rr[0, pl.ds(k, 1), :], rolled(v, -1, 0)),
            jnp.where(row == 0, rr[1, pl.ds(k, 1), :], rolled(v, 1, 0)),
        )

    arrive(cols_1)
    w2[12] = mixed(rp_1)

    def diffuse_body(block, carry):
        rim = w2[12]
        for i in range(2):
            k = block * 2 + i
            kf = level_of(k)
            h = heat_v[k]
            m = m0_v[k]
            h_around = around_of(h, rim, 127 - 2 * k, rr_1, k)
            m_around = around_of(m, rim, 127 - 2 * levels - 2 * k, rr_1, k + levels)
            h_sum, m_sum = h, m
            for f in range(4):
                w = jnp.where(w2[f] > kf, w2[4 + f], 0.0)
                h_sum = h_sum + w * (h_around[f] - h)
                m_sum = m_sum + w * (m_around[f] - m)
            t1_v[k] = jnp.where(code > kf, h_sum, 0.0)
            u_v[k] = m_sum
        return carry

    lax.fori_loop(0, levels // 2, diffuse_body, 0)

    shared(slots_1, recv_g, 1)
    coef = coefficients(totals(slots_1))
    surface_next = combined(coef, [own(v) for v in basis_1])
    back_one = combined([pltpu.roll(c, half, 1) for c in coef], basis_2)
    back_press = pressed(back_one)

    def reverse_body(block, total):
        for i in range(STEP):
            k = block * STEP + i
            kf = level_of(k)
            wet = code > kf
            second = t1_v[k] + jnp.where(
                wet, COUPLING * (1.0 - kf / levels) * surface_next, 0.0
            )
            t1_v[k] = second
            masked = jnp.where(
                wet,
                u_v[k]
                + (kf + 0.5) / levels * (1.0 + 2.0 * EOS_QUAD * second) * back_press,
                0.0,
            )
            m1_v[k] = masked
            total = total + COUPLING * (1.0 - kf / levels) * masked
        return total

    mine_c[0] = lax.fori_loop(0, levels // STEP, reverse_body, own(back_one))
    start(halo_c)
    packing(t1_v, m1_v, pack_2, row_2n, row_2s)
    start(cols_2)

    arrive(halo_c)
    basis_3, sums_3 = basis(wide(mine_c, ew_c, d_c, 0))
    vec_2[...] = gathered(sums_3, list(range(ENTRIES)))
    share(vec_2, slots_2, 2)

    arrive(cols_2)
    w2[13] = mixed(rp_2)

    def gradient_body(k, total):
        kf = level_of(k)
        h, m0, t, m1 = heat_v[k], m0_v[k], t1_v[k], m1_v[k]
        shift = 127 - 2 * k
        far = shift - 2 * levels
        h_around = around_of(h, w2[12], shift, rr_1, k)
        m0_around = around_of(m0, w2[12], far, rr_1, k + levels)
        t_around = around_of(t, w2[13], shift, rr_2, k)
        m1_around = around_of(m1, w2[13], far, rr_2, k + levels)
        spread = m1
        for f in range(4):
            wet = w2[f] > kf
            step = m1_around[f] - m1
            spread = spread + jnp.where(wet, w2[4 + f], 0.0) * step
            total = total + jnp.where(
                wet, (h_around[f] - h) * step + (t_around[f] - t) * (m0_around[f] - m0), 0.0
            )
        u_v[k] = spread
        return total

    diff_ref[...] = -0.5 * lax.fori_loop(0, levels, gradient_body, zero)

    shared(slots_2, recv_g, 2)
    surface = combined(coefficients(totals(slots_2)), basis_3)
    surface_ref[...] = own(surface)
    last_press = pressed(surface)

    def final_body(block, carry):
        for i in range(STEP):
            k = block * STEP + i
            kf = level_of(k)
            out_ref[k] = u_v[k] + jnp.where(
                code > kf,
                (kf + 0.5) / levels * (1.0 + 2.0 * EOS_QUAD * heat_v[k]) * last_press,
                0.0,
            )
        return carry

    lax.fori_loop(0, levels // STEP, final_body, 0)

    for copies in (halo_a, halo_b, halo_c, cols_1, cols_2):
        sent(copies)
    for turn, slots in enumerate((slots_0, slots_1, slots_2)):
        shared(slots, send_g, turn)


def shards(group, *args):
    heat, height = args[0], args[1]
    levels, rows, lanes = heat.shape
    f32 = jnp.float32
    cube = pltpu.VMEM((levels, rows, lanes), f32)

    def halos(fields):
        return [
            pltpu.VMEM((fields, rows, lanes), f32),
            pltpu.VMEM((2, fields, rows, lanes), f32),
            pltpu.VMEM((6, fields, RIM, lanes), f32),
        ]

    columns = [
        pltpu.VMEM((rows, lanes), f32),
        pltpu.VMEM((2, rows, lanes), f32),
        pltpu.VMEM((2 * levels, lanes), f32),
        pltpu.VMEM((2 * levels, lanes), f32),
        pltpu.VMEM((2, 2 * levels, lanes), f32),
    ]
    sums = [pltpu.VMEM((1, lanes), f32), pltpu.VMEM((group, 1, lanes), f32)]
    vmem = pl.BlockSpec(memory_space=pltpu.VMEM)
    hbm = pl.BlockSpec(memory_space=pl.ANY)
    return pl.pallas_call(
        kernel,
        out_shape=(
            jax.ShapeDtypeStruct(heat.shape, f32),
            jax.ShapeDtypeStruct(height.shape, f32),
            jax.ShapeDtypeStruct(height.shape, f32),
        ),
        in_specs=[hbm, vmem, hbm, vmem, vmem, vmem, vmem],
        out_specs=(vmem, vmem, vmem),
        scratch_shapes=[cube] * 6
        + [pltpu.VMEM((14, rows, lanes), f32)]
        + halos(3)
        + halos(2)
        + halos(1)
        + columns
        + columns
        + sums * 3
        + [
            pltpu.SemaphoreType.DMA((2,)),
            pltpu.SemaphoreType.DMA((24,)),
            pltpu.SemaphoreType.DMA((24,)),
            pltpu.SemaphoreType.DMA((8,)),
            pltpu.SemaphoreType.DMA((8,)),
            pltpu.SemaphoreType.DMA((3,)),
            pltpu.SemaphoreType.DMA((3,)),
        ],
        compiler_params=pltpu.CompilerParams(
            collective_id=0, has_side_effects=True, vmem_limit_bytes=40 * 1024 * 1024
        ),
    )(*args)


def solution(mesh):
    group = mesh.shape["lon"] * mesh.shape["lat"]
    cube = P(None, ("member", "lat"), "lon")
    plane = P(("member", "lat"), "lon")
    fixed = P("lat", "lon")
    return jax.shard_map(
        functools.partial(shards, group),
        mesh=mesh,
        in_specs=(cube, plane, cube, plane, fixed, fixed, fixed),
        out_specs=(cube, plane, plane),
        check_vma=False,
    )
```

```python
import functools
import math

import jax
import jax.numpy as jnp
from jax import lax
from jax.experimental import pallas as pl
from jax.experimental.pallas import tpu as pltpu
from jax.sharding import PartitionSpec as P

EOS_QUAD = 0.1
PRESS_COEF = 0.5
SURF_COEF = 4.0
COUPLING = 1.0

MESH = pl.DeviceIdType.MESH
RIM = 16
CHUNKS = 4
STEP = 4
SHIFT = 1.2
LINK = 0.2
ENTRIES = 11
WAYS = ((1, 0), (-1, 0), (0, 1), (0, -1), (1, 1), (-1, 1), (1, -1), (-1, -1))
BACK = tuple(WAYS.index((-a, -b)) for a, b in WAYS)


def rolled(x, shift, axis):
    return pltpu.roll(x, shift % x.shape[axis], axis)


def kernel(
    heat_hbm, height_hbm, closing_hbm, closing_height_hbm, mixing_hbm, sea_hbm, layers_hbm,
    out_ref, surface_ref, diff_ref,
    height, closing_height, mixing, sea, layers,
    heat_v, closing_v, m0_v, t1_v, u_v, m1_v, w2,
    mine_a, ew_a, d_a, mine_b, ew_b, d_b, mine_c, ew_c, d_c,
    pack_1, rp_1, row_1n, row_1s, rr_1, pack_2, rp_2, row_2n, row_2s, rr_2,
    vec_0, slots_0, vec_1, slots_1, vec_2, slots_2,
    load_sem, send_h, recv_h, send_p, recv_p, send_g, recv_g,
):
    levels, rows, lanes = heat_v.shape
    n_lon, n_lat = lax.axis_size("lon"), lax.axis_size("lat")
    group = n_lon * n_lat
    lon, lat = lax.axis_index("lon"), lax.axis_index("lat")
    me = lat * n_lon + lon

    loads = [
        pltpu.make_async_copy(src, dst, load_sem.at[i])
        for i, (src, dst) in enumerate(
            (
                (sea_hbm, sea),
                (layers_hbm, layers),
                (mixing_hbm, mixing),
                (height_hbm, height),
                (closing_height_hbm, closing_height),
            )
        )
    ]
    chunk = levels // CHUNKS
    cube_loads = [
        [
            pltpu.make_async_copy(
                src.at[pl.ds(c * chunk, chunk)],
                dst.at[pl.ds(c * chunk, chunk)],
                load_sem.at[5 + 2 * c + i],
            )
            for i, (src, dst) in enumerate(((heat_hbm, heat_v), (closing_hbm, closing_v)))
        ]
        for c in range(CHUNKS)
    ]
    for load in loads + sum(cube_loads, []):
        load.start()

    def peer(index):
        return {"lon": lax.rem(index, n_lon), "lat": lax.div(index, n_lon)}

    barrier = pltpu.get_barrier_semaphore()

    def greet(step, carry):
        pl.semaphore_signal(
            barrier, inc=1, device_id=peer(lax.rem(me + step, group)), device_id_type=MESH
        )
        return carry

    lax.fori_loop(1, group, greet, 0)

    def there(way):
        if WAYS[way][1] == 1:
            return lat < n_lat - 1
        if WAYS[way][1] == -1:
            return lat > 0
        return None

    def when(cond, action):
        if cond is None:
            action()
        else:
            pl.when(cond)(action)

    def target(way):
        return {
            "lon": lax.rem(lon + WAYS[way][0] + n_lon, n_lon),
            "lat": lat + WAYS[way][1],
        }

    def clear_south():
        for ref in (d_a, d_b, d_c):
            for slot in (1, 4, 5):
                ref[slot] = jnp.zeros(ref.shape[1:], jnp.float32)
        for ref in (rr_1, rr_2):
            ref[1] = jnp.zeros(ref.shape[1:], jnp.float32)

    def clear_north():
        for ref in (d_a, d_b, d_c):
            for slot in (0, 2, 3):
                ref[slot] = jnp.zeros(ref.shape[1:], jnp.float32)
        for ref in (rr_1, rr_2):
            ref[0] = jnp.zeros(ref.shape[1:], jnp.float32)

    pl.when(lat == 0)(clear_south)
    pl.when(lat == n_lat - 1)(clear_north)

    def halo(mine, ew, d, turn):
        copies = []
        for way in range(8):
            slot = BACK[way]
            if way < 2:
                src, dst = mine, ew.at[slot]
            else:
                first = rows - RIM if WAYS[way][1] == 1 else 0
                src, dst = mine.at[:, pl.ds(first, RIM), :], d.at[slot - 2]
            copies.append(
                pltpu.make_async_remote_copy(
                    src_ref=src,
                    dst_ref=dst,
                    send_sem=send_h.at[turn * 8 + way],
                    recv_sem=recv_h.at[turn * 8 + slot],
                    device_id=target(way),
                    device_id_type=MESH,
                )
            )
        return copies

    def columns(pack, rp, row_n, row_s, rr, turn):
        copies = []
        for way in range(4):
            slot = BACK[way]
            src = (pack, pack, row_n, row_s)[way]
            dst = rp.at[slot] if way < 2 else rr.at[slot - 2]
            copies.append(
                pltpu.make_async_remote_copy(
                    src_ref=src,
                    dst_ref=dst,
                    send_sem=send_p.at[turn * 4 + way],
                    recv_sem=recv_p.at[turn * 4 + slot],
                    device_id=target(way),
                    device_id_type=MESH,
                )
            )
        return copies

    def start(copies):
        for way, copy in enumerate(copies):
            when(there(way), copy.start)

    def arrive(copies):
        for way, copy in enumerate(copies):
            when(there(BACK[way]), copy.wait_recv)

    def sent(copies):
        for way, copy in enumerate(copies):
            when(there(way), copy.wait_send)

    def share(vec, slots, turn):
        def one(step, carry):
            pltpu.make_async_remote_copy(
                src_ref=vec,
                dst_ref=slots.at[me],
                send_sem=send_g.at[turn],
                recv_sem=recv_g.at[turn],
                device_id=peer(lax.rem(me + step, group)),
                device_id_type=MESH,
            ).start()
            return carry

        slots[me] = vec[...]
        lax.fori_loop(1, group, one, 0)

    def shared(slots, sem, turn):
        several = slots.at[pl.ds(0, group - 1)]
        pltpu.make_async_copy(several, several, sem.at[turn]).wait()

    halo_a = halo(mine_a, ew_a, d_a, 0)
    halo_b = halo(mine_b, ew_b, d_b, 1)
    halo_c = halo(mine_c, ew_c, d_c, 2)
    cols_1 = columns(pack_1, rp_1, row_1n, row_1s, rr_1, 0)
    cols_2 = columns(pack_2, rp_2, row_2n, row_2s, rr_2, 1)

    lane = lax.broadcasted_iota(jnp.int32, (rows, lanes), 1)
    row = lax.broadcasted_iota(jnp.int32, (rows, lanes), 0)
    lane_8 = lax.broadcasted_iota(jnp.int32, (8, lanes), 1)
    sub_8 = lax.broadcasted_iota(jnp.int32, (8, lanes), 0)

    for load in loads[:4]:
        load.wait()
    code = (sea[...] * layers[...]).astype(jnp.float32)
    mine_a[0] = code
    mine_a[1] = mixing[...]
    mine_a[2] = height[...]

    def folded(x):
        total = x[0:8]
        for i in range(8, x.shape[0], 8):
            total = total + x[i : i + 8]
        return jnp.sum(total, axis=0, keepdims=True)

    def gathered(sums, places):
        result = jnp.zeros((1, lanes), jnp.float32)
        for first in range(0, len(sums), 8):
            some = sums[first : first + 8]
            table = jnp.zeros((8, lanes), jnp.float32)
            spot = jnp.full((8, lanes), -1, jnp.int32)
            for i, item in enumerate(some):
                table = jnp.where(sub_8 == i, item, table)
                spot = jnp.where(sub_8 == i, places[first + i], spot)
            column = jnp.sum(table, axis=1, keepdims=True)
            result = result + jnp.sum(
                jnp.where(lane_8 == spot, column, 0.0), axis=0, keepdims=True
            )
        return result

    share_of = code * (SURF_COEF / levels)
    east = jnp.minimum(share_of, rolled(share_of, -1, 1))
    north = jnp.minimum(share_of, rolled(share_of, -1, 0))
    diagonal = east + rolled(east, 1, 1) + north + rolled(north, 1, 0)
    second_moment = diagonal * diagonal + 2.0 * (east * east + north * north)
    vec_0[...] = gathered([folded(diagonal), folded(second_moment)], [0, 1])

    pl.semaphore_wait(barrier, group - 1)
    start(halo_a)
    share(vec_0, slots_0, 0)


    def level_of(k):
        return k.astype(jnp.float32)

    def load_body(block, carry):
        press, total = carry
        for i in range(STEP):
            k = block * STEP + i
            kf = level_of(k)
            h = heat_v[k]
            wet = code > kf
            masked = jnp.where(wet, closing_v[k], 0.0)
            m0_v[k] = masked
            press = press + jnp.where(
                wet, (kf + 0.5) / levels * (h + EOS_QUAD * h * h), 0.0
            )
            total = total + COUPLING * (1.0 - kf / levels) * masked
        return press, total

    zero = jnp.zeros((rows, lanes), jnp.float32)
    loads[4].wait()
    carry = (zero, closing_height[...])
    for c in range(CHUNKS):
        for load in cube_loads[c]:
            load.wait()
        first = c * chunk // STEP
        carry = lax.fori_loop(first, first + chunk // STEP, load_body, carry)
    press, total_one = carry
    mine_b[0] = press / math.sqrt(levels)
    mine_b[1] = total_one
    start(halo_b)

    def pack_level(k, a, b, packed, row_n, row_s):
        packed = jnp.where((lane >> 1) == k, pltpu.roll(a, 2 * k + 1, 1), packed)
        packed = jnp.where(
            (lane >> 1) == k + levels, pltpu.roll(b, 2 * k + 2 * levels + 1, 1), packed
        )
        row_n[pl.ds(k, 1), :] = a[rows - 1 : rows, :]
        row_n[pl.ds(k + levels, 1), :] = b[rows - 1 : rows, :]
        row_s[pl.ds(k, 1), :] = a[0:1, :]
        row_s[pl.ds(k + levels, 1), :] = b[0:1, :]
        return packed

    def pack_body(block, packed):
        for i in range(STEP):
            k = block * STEP + i
            packed = pack_level(k, heat_v[k], m0_v[k], packed, row_1n, row_1s)
        return packed

    pack_1[...] = lax.fori_loop(0, levels // STEP, pack_body, zero)
    start(cols_1)

    def wide(mine, ew, d, f):
        half = lax.broadcasted_iota(jnp.int32, (rows, lanes), 1) < lanes // 2
        half_8 = lax.broadcasted_iota(jnp.int32, (RIM, lanes), 1) < lanes // 2
        left = jnp.concatenate([mine[f], d[0, f], d[1, f]], axis=0)
        right = jnp.concatenate(
            [
                jnp.where(half, ew[0, f], ew[1, f]),
                jnp.where(half_8, d[2, f], d[3, f]),
                jnp.where(half_8, d[4, f], d[5, f]),
            ],
            axis=0,
        )
        return jnp.concatenate([left, right], axis=1)

    def own(x):
        return x[:rows, :lanes]

    def sides(x):
        return rolled(x, -1, 1), rolled(x, 1, 1), rolled(x, -1, 0), rolled(x, 1, 0)

    arrive(halo_a)
    code_w = wide(mine_a, ew_a, d_a, 0)
    mix_w = wide(mine_a, ew_a, d_a, 1)
    height_w = wide(mine_a, ew_a, d_a, 2)
    near_code = [jnp.minimum(code_w, x) for x in sides(code_w)]
    for i, x in enumerate(near_code):
        w2[i] = own(x)
    for i, x in enumerate(sides(mix_w)):
        w2[4 + i] = own(0.5 * (mix_w + x))
    face_land = [jnp.where(x > 0.0, 1.0, 0.0) for x in near_code]
    for i, x in enumerate(face_land):
        w2[8 + i] = own(x) * PRESS_COEF

    def totals(slots):
        return jnp.broadcast_to(jnp.sum(slots[...], axis=0), (8, lanes))

    def at(total, entry):
        return pltpu.roll(total, (lanes - entry) % lanes, 1)

    def scalar(x):
        return x[0:1, 0:1]

    shared(slots_0, recv_g, 0)
    moments = totals(slots_0)
    trace = at(moments, 0)
    ratio = jnp.where(trace > 0.0, at(moments, 1) / jnp.where(trace > 0.0, trace, 1.0), 1.0)
    scale = jnp.where(lane_8 < lanes // 2, ratio, pltpu.roll(ratio, lanes // 2, 1))
    weight = scalar(1.0 / scale) * (SURF_COEF / levels)
    solver_w = [x * weight for x in near_code]

    def apply(v):
        around = sides(v)
        result = solver_w[0] * (v - around[0])
        for w, x in zip(solver_w[1:], around[1:]):
            result = result + w * (v - x)
        return result

    def basis(b):
        v1 = apply(b)
        v2 = apply(v1) - SHIFT * v1
        v3 = apply(v2) - SHIFT * v2 - LINK * v1
        v4 = own(apply(v3))
        o = [own(v) for v in (b, v1, v2, v3)]
        pairs = ((0, 0), (0, 1), (0, 2), (0, 3), (1, 1), (1, 2), (1, 3), (2, 2), (2, 3), (3, 3))
        sums = [folded(o[i] * o[j]) for i, j in pairs] + [folded(o[3] * v4)]
        return (b, v1, v2, v3), sums

    def coefficients(total):
        g00, g01, g02, g03, g11, g12, g13, g22, g23, g33, g34 = [
            at(total, e) for e in range(ENTRIES)
        ]
        m = {
            (0, 0): g00 + scale * g01,
            (0, 1): g01 + scale * g11,
            (0, 2): g02 + scale * g12,
            (0, 3): g03 + scale * g13,
            (1, 1): g11 + scale * (g12 + SHIFT * g11),
            (1, 2): g12 + scale * (g22 + SHIFT * g12),
            (1, 3): g13 + scale * (g23 + SHIFT * g13),
            (2, 2): g22 + scale * (g23 + SHIFT * g22 + LINK * g12),
            (2, 3): g23 + scale * (g33 + SHIFT * g23 + LINK * g13),
            (3, 3): g33 + scale * g34,
        }
        c = [g00, g01, g02, g03]
        low, inverse = {}, []
        work = dict(m)
        for j in range(4):
            pivot = work[j, j]
            good = pivot > 3e-7 * m[j, j]
            inv = jnp.where(good, 1.0 / jnp.where(good, pivot, 1.0), 0.0)
            inverse.append(inv)
            for i in range(j + 1, 4):
                low[i, j] = work[j, i] * inv
            for i in range(j + 1, 4):
                for k in range(i, 4):
                    work[i, k] = work[i, k] - low[i, j] * work[j, k]
                c[i] = c[i] - low[i, j] * c[j]
        c = [x * inv for x, inv in zip(c, inverse)]
        for i in (2, 1, 0):
            for j in range(i + 1, 4):
                c[i] = c[i] - low[j, i] * c[j]
        return c

    def combined(c, vs):
        result = scalar(c[0]) * vs[0]
        for a, v in zip(c[1:], vs[1:]):
            result = result + scalar(a) * v
        return result

    def pressed_wide(x):
        result = 0.0
        for w, y in zip(face_land, sides(x)):
            result = result + (PRESS_COEF / math.sqrt(levels)) * w * (x - y)
        return result

    def pressed(x):
        around = sides(x)
        centre = own(x)
        result = w2[8] * (centre - own(around[0]))
        for i in range(1, 4):
            result = result + w2[8 + i] * (centre - own(around[i]))
        return result * (1.0 / math.sqrt(levels))

    arrive(halo_b)
    press_w = wide(mine_b, ew_b, d_b, 0)
    rhs = height_w
    for w, x in zip(face_land, sides(press_w)):
        rhs = rhs + (PRESS_COEF * w) * (press_w - x)
    basis_1, sums_1 = basis(rhs)
    basis_2, sums_2 = basis(wide(mine_b, ew_b, d_b, 1))
    half = lanes // 2
    vec_1[...] = gathered(
        sums_1 + sums_2, list(range(ENTRIES)) + [half + e for e in range(ENTRIES)]
    )
    share(vec_1, slots_1, 1)

    def mixed(rp):
        return jnp.where((lane & 1) == 0, rolled(rp[0], -1, 1), rolled(rp[1], 1, 1))

    def around_of(v, rim, shift, rr, k):
        r = pltpu.roll(rim, shift, 1)
        return (
            jnp.where(lane == lanes - 1, r, rolled(v, -1, 1)),
            jnp.where(lane == 0, r, rolled(v, 1, 1)),
            jnp.where(row == rows - 1, rr[0, pl.ds(k, 1), :], rolled(v, -1, 0)),
            jnp.where(row == 0, rr[1, pl.ds(k, 1), :], rolled(v, 1, 0)),
        )

    both = jnp.zeros_like(code_w)
    for k in range(levels):
        part = COUPLING**2 * (1.0 - k / levels) ** 2 * (k + 0.5) / levels * 2.0 * EOS_QUAD
        both = both + jnp.where(code_w > float(k), part, 0.0)

    arrive(cols_1)
    w2[12] = mixed(rp_1)

    def diffuse_body(block, carry):
        plain, scaled = carry
        rim = w2[12]
        for i in range(2):
            k = block * 2 + i
            kf = level_of(k)
            h = heat_v[k]
            m = m0_v[k]
            h_around = around_of(h, rim, 127 - 2 * k, rr_1, k)
            m_around = around_of(m, rim, 127 - 2 * levels - 2 * k, rr_1, k + levels)
            h_sum, m_sum = h, m
            for f in range(4):
                w = jnp.where(w2[f] > kf, w2[4 + f], 0.0)
                h_sum = h_sum + w * (h_around[f] - h)
                m_sum = m_sum + w * (m_around[f] - m)
            wet = code > kf
            h_sum = jnp.where(wet, h_sum, 0.0)
            t1_v[k] = h_sum
            u_v[k] = m_sum
            profile = COUPLING * (1.0 - kf / levels)
            plain = plain + jnp.where(wet, profile * m_sum, 0.0)
            scaled = scaled + jnp.where(
                wet,
                profile * (kf + 0.5) / levels * (1.0 + 2.0 * EOS_QUAD * h_sum),
                0.0,
            )
        return plain, scaled

    plain, scaled = lax.fori_loop(0, levels // 2, diffuse_body, (zero, zero))
    mine_c[0] = plain
    mine_c[1] = scaled
    start(halo_c)

    shared(slots_1, recv_g, 1)
    coef = coefficients(totals(slots_1))
    surface_w = combined(coef, basis_1)
    back_one = combined([pltpu.roll(c, half, 1) for c in coef], basis_2)
    back_press_w = pressed_wide(back_one)

    arrive(halo_c)
    total_zero = (
        back_one
        + wide(mine_c, ew_c, d_c, 0)
        + back_press_w * (wide(mine_c, ew_c, d_c, 1) + both * surface_w)
    )
    basis_3, sums_3 = basis(total_zero)
    vec_2[...] = gathered(sums_3, list(range(ENTRIES)))
    share(vec_2, slots_2, 2)

    surface_next = own(surface_w)
    back_press = own(back_press_w)

    def reverse_body(block, packed):
        for i in range(STEP):
            k = block * STEP + i
            kf = level_of(k)
            wet = code > kf
            second = t1_v[k] + jnp.where(
                wet, COUPLING * (1.0 - kf / levels) * surface_next, 0.0
            )
            masked = jnp.where(
                wet,
                u_v[k]
                + (kf + 0.5) / levels * (1.0 + 2.0 * EOS_QUAD * second) * back_press,
                0.0,
            )
            t1_v[k] = second
            m1_v[k] = masked
            packed = pack_level(k, second, masked, packed, row_2n, row_2s)
        return packed

    pack_2[...] = lax.fori_loop(0, levels // STEP, reverse_body, zero)
    start(cols_2)

    arrive(cols_2)
    w2[13] = mixed(rp_2)

    def gradient_body(k, total):
        kf = level_of(k)
        h, m0, t, m1 = heat_v[k], m0_v[k], t1_v[k], m1_v[k]
        shift = 127 - 2 * k
        far = shift - 2 * levels
        h_around = around_of(h, w2[12], shift, rr_1, k)
        m0_around = around_of(m0, w2[12], far, rr_1, k + levels)
        t_around = around_of(t, w2[13], shift, rr_2, k)
        m1_around = around_of(m1, w2[13], far, rr_2, k + levels)
        spread = m1
        for f in range(4):
            wet = w2[f] > kf
            step = m1_around[f] - m1
            spread = spread + jnp.where(wet, w2[4 + f], 0.0) * step
            total = total + jnp.where(
                wet, (h_around[f] - h) * step + (t_around[f] - t) * (m0_around[f] - m0), 0.0
            )
        u_v[k] = spread
        return total

    diff_ref[...] = -0.5 * lax.fori_loop(0, levels, gradient_body, zero)

    shared(slots_2, recv_g, 2)
    surface = combined(coefficients(totals(slots_2)), basis_3)
    surface_ref[...] = own(surface)
    last_press = pressed(surface)

    def final_body(block, carry):
        for i in range(STEP):
            k = block * STEP + i
            kf = level_of(k)
            out_ref[k] = u_v[k] + jnp.where(
                code > kf,
                (kf + 0.5) / levels * (1.0 + 2.0 * EOS_QUAD * heat_v[k]) * last_press,
                0.0,
            )
        return carry

    lax.fori_loop(0, levels // STEP, final_body, 0)

    for copies in (halo_a, halo_b, halo_c, cols_1, cols_2):
        sent(copies)
    for turn, slots in enumerate((slots_0, slots_1, slots_2)):
        shared(slots, send_g, turn)


def shards(group, *args):
    heat, height = args[0], args[1]
    levels, rows, lanes = heat.shape
    f32 = jnp.float32
    cube = pltpu.VMEM((levels, rows, lanes), f32)
    plane = pltpu.VMEM((rows, lanes), f32)

    def halos(fields):
        return [
            pltpu.VMEM((fields, rows, lanes), f32),
            pltpu.VMEM((2, fields, rows, lanes), f32),
            pltpu.VMEM((6, fields, RIM, lanes), f32),
        ]

    columns = [
        pltpu.VMEM((rows, lanes), f32),
        pltpu.VMEM((2, rows, lanes), f32),
        pltpu.VMEM((2 * levels, lanes), f32),
        pltpu.VMEM((2 * levels, lanes), f32),
        pltpu.VMEM((2, 2 * levels, lanes), f32),
    ]
    sums = [pltpu.VMEM((1, lanes), f32), pltpu.VMEM((group, 1, lanes), f32)]
    vmem = pl.BlockSpec(memory_space=pltpu.VMEM)
    hbm = pl.BlockSpec(memory_space=pltpu.HBM)
    return pl.pallas_call(
        kernel,
        out_shape=(
            jax.ShapeDtypeStruct(heat.shape, f32),
            jax.ShapeDtypeStruct(height.shape, f32),
            jax.ShapeDtypeStruct(height.shape, f32),
        ),
        in_specs=[hbm] * 7,
        out_specs=(vmem, vmem, vmem),
        scratch_shapes=[plane] * 3
        + [pltpu.VMEM((rows, lanes), jnp.int32)] * 2
        + [cube] * 6
        + [pltpu.VMEM((14, rows, lanes), f32)]
        + halos(3)
        + halos(2)
        + halos(2)
        + columns
        + columns
        + sums * 3
        + [
            pltpu.SemaphoreType.DMA((5 + 2 * CHUNKS,)),
            pltpu.SemaphoreType.DMA((24,)),
            pltpu.SemaphoreType.DMA((24,)),
            pltpu.SemaphoreType.DMA((8,)),
            pltpu.SemaphoreType.DMA((8,)),
            pltpu.SemaphoreType.DMA((3,)),
            pltpu.SemaphoreType.DMA((3,)),
        ],
        compiler_params=pltpu.CompilerParams(
            collective_id=0, has_side_effects=True, vmem_limit_bytes=58 * 1024 * 1024
        ),
    )(*args)


def solution(mesh):
    group = mesh.shape["lon"] * mesh.shape["lat"]
    cube = P(None, ("member", "lat"), "lon")
    plane = P(("member", "lat"), "lon")
    fixed = P("lat", "lon")
    return jax.shard_map(
        functools.partial(shards, group),
        mesh=mesh,
        in_specs=(cube, plane, cube, plane, fixed, fixed, fixed),
        out_specs=(cube, plane, plane),
        check_vma=False,
    )
```

```python
import functools
import math

import jax
import jax.numpy as jnp
from jax import lax
from jax.experimental import pallas as pl
from jax.experimental.pallas import tpu as pltpu
from jax.sharding import PartitionSpec as P

EOS_QUAD = 0.1
PRESS_COEF = 0.5
SURF_COEF = 4.0
COUPLING = 1.0

MESH = pl.DeviceIdType.MESH
RIM = 8
CHUNKS = 4
STEP = 8
SHIFT = 1.2
LINK = 0.2
ENTRIES = 11
WAYS = ((1, 0), (-1, 0), (0, 1), (0, -1), (1, 1), (-1, 1), (1, -1), (-1, -1))
BACK = tuple(WAYS.index((-a, -b)) for a, b in WAYS)


def rolled(x, shift, axis):
    return pltpu.roll(x, shift % x.shape[axis], axis)


def kernel(
    heat_hbm, height_hbm, closing_hbm, closing_height_hbm, mixing_hbm, sea_hbm, layers_hbm,
    out_ref, surface_ref, diff_ref,
    height, closing_height, mixing, sea, layers,
    heat_v, closing_v, m0_v, t1_v, u_v, m1_v, w2,
    mine_a, ew_a, d_a, mine_b, ew_b, d_b, mine_c, ew_c, d_c,
    pack_1, rp_1, row_1n, row_1s, rr_1, pack_2, rp_2, row_2n, row_2s, rr_2,
    vec_0, slots_0, vec_1, slots_1, vec_2, slots_2,
    load_sem, send_h, recv_h, send_p, recv_p, send_g, recv_g,
):
    levels, rows, lanes = heat_v.shape
    n_lon, n_lat = lax.axis_size("lon"), lax.axis_size("lat")
    group = n_lon * n_lat
    lon, lat = lax.axis_index("lon"), lax.axis_index("lat")
    me = lat * n_lon + lon

    loads = [
        pltpu.make_async_copy(src, dst, load_sem.at[i])
        for i, (src, dst) in enumerate(
            (
                (sea_hbm, sea),
                (layers_hbm, layers),
                (mixing_hbm, mixing),
                (height_hbm, height),
                (closing_height_hbm, closing_height),
            )
        )
    ]
    chunk = levels // CHUNKS
    cube_loads = [
        [
            pltpu.make_async_copy(
                src.at[pl.ds(c * chunk, chunk)],
                dst.at[pl.ds(c * chunk, chunk)],
                load_sem.at[5 + 2 * c + i],
            )
            for i, (src, dst) in enumerate(((heat_hbm, heat_v), (closing_hbm, closing_v)))
        ]
        for c in range(CHUNKS)
    ]
    for load in loads + sum(cube_loads, []):
        load.start()

    def peer(index):
        return {"lon": lax.rem(index, n_lon), "lat": lax.div(index, n_lon)}

    barrier = pltpu.get_barrier_semaphore()

    def greet(step, carry):
        pl.semaphore_signal(
            barrier, inc=1, device_id=peer(lax.rem(me + step, group)), device_id_type=MESH
        )
        return carry

    lax.fori_loop(1, group, greet, 0)

    def there(way):
        if WAYS[way][1] == 1:
            return lat < n_lat - 1
        if WAYS[way][1] == -1:
            return lat > 0
        return None

    def when(cond, action):
        if cond is None:
            action()
        else:
            pl.when(cond)(action)

    def target(way):
        return {
            "lon": lax.rem(lon + WAYS[way][0] + n_lon, n_lon),
            "lat": lat + WAYS[way][1],
        }

    def clear_south():
        for ref in (d_a, d_b, d_c):
            for slot in (1, 4, 5):
                ref[slot] = jnp.zeros(ref.shape[1:], jnp.float32)
        for ref in (rr_1, rr_2):
            ref[1] = jnp.zeros(ref.shape[1:], jnp.float32)

    def clear_north():
        for ref in (d_a, d_b, d_c):
            for slot in (0, 2, 3):
                ref[slot] = jnp.zeros(ref.shape[1:], jnp.float32)
        for ref in (rr_1, rr_2):
            ref[0] = jnp.zeros(ref.shape[1:], jnp.float32)

    pl.when(lat == 0)(clear_south)
    pl.when(lat == n_lat - 1)(clear_north)

    def halo(mine, ew, d, turn):
        copies = []
        for way in range(8):
            slot = BACK[way]
            if way < 2:
                src, dst = mine, ew.at[slot]
            else:
                first = rows - RIM if WAYS[way][1] == 1 else 0
                src, dst = mine.at[:, pl.ds(first, RIM), :], d.at[slot - 2]
            copies.append(
                pltpu.make_async_remote_copy(
                    src_ref=src,
                    dst_ref=dst,
                    send_sem=send_h.at[turn * 8 + way],
                    recv_sem=recv_h.at[turn * 8 + slot],
                    device_id=target(way),
                    device_id_type=MESH,
                )
            )
        return copies

    def columns(pack, rp, row_n, row_s, rr, turn):
        copies = []
        for way in range(4):
            slot = BACK[way]
            src = (pack, pack, row_n, row_s)[way]
            dst = rp.at[slot] if way < 2 else rr.at[slot - 2]
            copies.append(
                pltpu.make_async_remote_copy(
                    src_ref=src,
                    dst_ref=dst,
                    send_sem=send_p.at[turn * 4 + way],
                    recv_sem=recv_p.at[turn * 4 + slot],
                    device_id=target(way),
                    device_id_type=MESH,
                )
            )
        return copies

    def start(copies):
        for way, copy in enumerate(copies):
            when(there(way), copy.start)

    def arrive(copies):
        for way, copy in enumerate(copies):
            when(there(BACK[way]), copy.wait_recv)

    def sent(copies):
        for way, copy in enumerate(copies):
            when(there(way), copy.wait_send)

    def share(vec, slots, turn):
        def one(step, carry):
            pltpu.make_async_remote_copy(
                src_ref=vec,
                dst_ref=slots.at[me],
                send_sem=send_g.at[turn],
                recv_sem=recv_g.at[turn],
                device_id=peer(lax.rem(me + step, group)),
                device_id_type=MESH,
            ).start()
            return carry

        slots[me] = vec[...]
        lax.fori_loop(1, group, one, 0)

    def shared(slots, sem, turn):
        several = slots.at[pl.ds(0, group - 1)]
        pltpu.make_async_copy(several, several, sem.at[turn]).wait()

    halo_a = halo(mine_a, ew_a, d_a, 0)
    halo_b = halo(mine_b, ew_b, d_b, 1)
    halo_c = halo(mine_c, ew_c, d_c, 2)
    cols_1 = columns(pack_1, rp_1, row_1n, row_1s, rr_1, 0)
    cols_2 = columns(pack_2, rp_2, row_2n, row_2s, rr_2, 1)

    lane = lax.broadcasted_iota(jnp.int32, (rows, lanes), 1)
    row = lax.broadcasted_iota(jnp.int32, (rows, lanes), 0)
    lane_8 = lax.broadcasted_iota(jnp.int32, (8, lanes), 1)
    sub_8 = lax.broadcasted_iota(jnp.int32, (8, lanes), 0)

    for load in loads[:4]:
        load.wait()
    code = (sea[...] * layers[...]).astype(jnp.float32)
    mine_a[0] = code
    mine_a[1] = mixing[...]
    mine_a[2] = height[...]

    def folded(x):
        total = x[0:8]
        for i in range(8, x.shape[0], 8):
            total = total + x[i : i + 8]
        return jnp.sum(total, axis=0, keepdims=True)

    def gathered(sums, places):
        result = jnp.zeros((1, lanes), jnp.float32)
        for first in range(0, len(sums), 8):
            some = sums[first : first + 8]
            table = jnp.zeros((8, lanes), jnp.float32)
            spot = jnp.full((8, lanes), -1, jnp.int32)
            for i, item in enumerate(some):
                table = jnp.where(sub_8 == i, item, table)
                spot = jnp.where(sub_8 == i, places[first + i], spot)
            column = jnp.sum(table, axis=1, keepdims=True)
            result = result + jnp.sum(
                jnp.where(lane_8 == spot, column, 0.0), axis=0, keepdims=True
            )
        return result

    share_of = code * (SURF_COEF / levels)
    east = jnp.minimum(share_of, rolled(share_of, -1, 1))
    north = jnp.minimum(share_of, rolled(share_of, -1, 0))
    diagonal = east + rolled(east, 1, 1) + north + rolled(north, 1, 0)
    second_moment = diagonal * diagonal + 2.0 * (east * east + north * north)
    vec_0[...] = gathered([folded(diagonal), folded(second_moment)], [0, 1])

    pl.semaphore_wait(barrier, group - 1)
    start(halo_a)
    share(vec_0, slots_0, 0)


    def level_of(k):
        return k.astype(jnp.float32)

    def load_body(block, carry):
        press, total = carry
        for i in range(STEP):
            k = block * STEP + i
            kf = level_of(k)
            h = heat_v[k]
            wet = code > kf
            masked = jnp.where(wet, closing_v[k], 0.0)
            m0_v[k] = masked
            press = press + jnp.where(
                wet, (kf + 0.5) / levels * (h + EOS_QUAD * h * h), 0.0
            )
            total = total + COUPLING * (1.0 - kf / levels) * masked
        return press, total

    zero = jnp.zeros((rows, lanes), jnp.float32)
    loads[4].wait()
    carry = (zero, closing_height[...])
    for c in range(CHUNKS):
        for load in cube_loads[c]:
            load.wait()
        first = c * chunk // STEP
        carry = lax.fori_loop(first, first + chunk // STEP, load_body, carry)
    press, total_one = carry
    mine_b[0] = press / math.sqrt(levels)
    mine_b[1] = total_one
    start(halo_b)

    def pack_level(k, a, b, packed, row_n, row_s):
        packed = jnp.where((lane >> 1) == k, pltpu.roll(a, 2 * k + 1, 1), packed)
        packed = jnp.where(
            (lane >> 1) == k + levels, pltpu.roll(b, 2 * k + 2 * levels + 1, 1), packed
        )
        row_n[pl.ds(k, 1), :] = a[rows - 1 : rows, :]
        row_n[pl.ds(k + levels, 1), :] = b[rows - 1 : rows, :]
        row_s[pl.ds(k, 1), :] = a[0:1, :]
        row_s[pl.ds(k + levels, 1), :] = b[0:1, :]
        return packed

    def pack_body(block, packed):
        for i in range(STEP):
            k = block * STEP + i
            packed = pack_level(k, heat_v[k], m0_v[k], packed, row_1n, row_1s)
        return packed

    pack_1[...] = lax.fori_loop(0, levels // STEP, pack_body, zero)
    start(cols_1)

    def wide(mine, ew, d, f):
        half = lax.broadcasted_iota(jnp.int32, (rows, lanes), 1) < lanes // 2
        half_8 = lax.broadcasted_iota(jnp.int32, (RIM, lanes), 1) < lanes // 2
        left = jnp.concatenate([mine[f], d[0, f], d[1, f]], axis=0)
        right = jnp.concatenate(
            [
                jnp.where(half, ew[0, f], ew[1, f]),
                jnp.where(half_8, d[2, f], d[3, f]),
                jnp.where(half_8, d[4, f], d[5, f]),
            ],
            axis=0,
        )
        return jnp.concatenate([left, right], axis=1)

    def own(x):
        return x[:rows, :lanes]

    def sides(x):
        return rolled(x, -1, 1), rolled(x, 1, 1), rolled(x, -1, 0), rolled(x, 1, 0)

    arrive(halo_a)
    code_w = wide(mine_a, ew_a, d_a, 0)
    mix_w = wide(mine_a, ew_a, d_a, 1)
    height_w = wide(mine_a, ew_a, d_a, 2)
    near_code = [jnp.minimum(code_w, x) for x in sides(code_w)]
    for i, x in enumerate(near_code):
        w2[i] = own(x)
    for i, x in enumerate(sides(mix_w)):
        w2[4 + i] = own(0.5 * (mix_w + x))
    face_land = [jnp.where(x > 0.0, 1.0, 0.0) for x in near_code]
    for i, x in enumerate(face_land):
        w2[8 + i] = own(x) * PRESS_COEF

    def totals(slots):
        return jnp.broadcast_to(jnp.sum(slots[...], axis=0), (8, lanes))

    def at(total, entry):
        return pltpu.roll(total, (lanes - entry) % lanes, 1)

    def scalar(x):
        return x[0:1, 0:1]

    shared(slots_0, recv_g, 0)
    moments = totals(slots_0)
    trace = at(moments, 0)
    ratio = jnp.where(trace > 0.0, at(moments, 1) / jnp.where(trace > 0.0, trace, 1.0), 1.0)
    scale = jnp.where(lane_8 < lanes // 2, ratio, pltpu.roll(ratio, lanes // 2, 1))
    weight = scalar(1.0 / scale) * (SURF_COEF / levels)
    solver_w = [x * weight for x in near_code]

    def apply(v):
        around = sides(v)
        result = solver_w[0] * (v - around[0])
        for w, x in zip(solver_w[1:], around[1:]):
            result = result + w * (v - x)
        return result

    def basis(b):
        v1 = apply(b)
        v2 = apply(v1) - SHIFT * v1
        v3 = apply(v2) - SHIFT * v2 - LINK * v1
        v4 = own(apply(v3))
        o = [own(v) for v in (b, v1, v2, v3)]
        pairs = ((0, 0), (0, 1), (0, 2), (0, 3), (1, 1), (1, 2), (1, 3), (2, 2), (2, 3), (3, 3))
        sums = [folded(o[i] * o[j]) for i, j in pairs] + [folded(o[3] * v4)]
        return (b, v1, v2, v3), sums

    def coefficients(total):
        g00, g01, g02, g03, g11, g12, g13, g22, g23, g33, g34 = [
            at(total, e) for e in range(ENTRIES)
        ]
        m = {
            (0, 0): g00 + scale * g01,
            (0, 1): g01 + scale * g11,
            (0, 2): g02 + scale * g12,
            (0, 3): g03 + scale * g13,
            (1, 1): g11 + scale * (g12 + SHIFT * g11),
            (1, 2): g12 + scale * (g22 + SHIFT * g12),
            (1, 3): g13 + scale * (g23 + SHIFT * g13),
            (2, 2): g22 + scale * (g23 + SHIFT * g22 + LINK * g12),
            (2, 3): g23 + scale * (g33 + SHIFT * g23 + LINK * g13),
            (3, 3): g33 + scale * g34,
        }
        c = [g00, g01, g02, g03]
        low, inverse = {}, []
        work = dict(m)
        for j in range(4):
            pivot = work[j, j]
            good = pivot > 3e-7 * m[j, j]
            inv = jnp.where(good, 1.0 / jnp.where(good, pivot, 1.0), 0.0)
            inverse.append(inv)
            for i in range(j + 1, 4):
                low[i, j] = work[j, i] * inv
            for i in range(j + 1, 4):
                for k in range(i, 4):
                    work[i, k] = work[i, k] - low[i, j] * work[j, k]
                c[i] = c[i] - low[i, j] * c[j]
        c = [x * inv for x, inv in zip(c, inverse)]
        for i in (2, 1, 0):
            for j in range(i + 1, 4):
                c[i] = c[i] - low[j, i] * c[j]
        return c

    def combined(c, vs):
        result = scalar(c[0]) * vs[0]
        for a, v in zip(c[1:], vs[1:]):
            result = result + scalar(a) * v
        return result

    def pressed_wide(x):
        result = 0.0
        for w, y in zip(face_land, sides(x)):
            result = result + (PRESS_COEF / math.sqrt(levels)) * w * (x - y)
        return result

    def pressed(x):
        around = sides(x)
        centre = own(x)
        result = w2[8] * (centre - own(around[0]))
        for i in range(1, 4):
            result = result + w2[8 + i] * (centre - own(around[i]))
        return result * (1.0 / math.sqrt(levels))

    both = jnp.zeros_like(code_w)
    for k in range(levels):
        part = COUPLING**2 * (1.0 - k / levels) ** 2 * (k + 0.5) / levels * 2.0 * EOS_QUAD
        both = both + jnp.where(code_w > float(k), part, 0.0)

    arrive(halo_b)
    press_w = wide(mine_b, ew_b, d_b, 0)
    rhs = height_w
    for w, x in zip(face_land, sides(press_w)):
        rhs = rhs + (PRESS_COEF * w) * (press_w - x)
    basis_1, sums_1 = basis(rhs)
    basis_2, sums_2 = basis(wide(mine_b, ew_b, d_b, 1))
    half = lanes // 2
    vec_1[...] = gathered(
        sums_1 + sums_2, list(range(ENTRIES)) + [half + e for e in range(ENTRIES)]
    )
    share(vec_1, slots_1, 1)

    def mixed(rp):
        return jnp.where((lane & 1) == 0, rolled(rp[0], -1, 1), rolled(rp[1], 1, 1))

    def around_of(v, rim, shift, rr, k):
        r = pltpu.roll(rim, shift, 1)
        return (
            jnp.where(lane == lanes - 1, r, rolled(v, -1, 1)),
            jnp.where(lane == 0, r, rolled(v, 1, 1)),
            jnp.where(row == rows - 1, rr[0, pl.ds(k, 1), :], rolled(v, -1, 0)),
            jnp.where(row == 0, rr[1, pl.ds(k, 1), :], rolled(v, 1, 0)),
        )

    arrive(cols_1)
    w2[12] = mixed(rp_1)

    def diffuse_body(block, carry):
        plain, scaled = carry
        rim = w2[12]
        for i in range(STEP):
            k = block * STEP + i
            kf = level_of(k)
            h = heat_v[k]
            m = m0_v[k]
            h_around = around_of(h, rim, 127 - 2 * k, rr_1, k)
            m_around = around_of(m, rim, 127 - 2 * levels - 2 * k, rr_1, k + levels)
            h_sum, m_sum = h, m
            for f in range(4):
                w = jnp.where(w2[f] > kf, w2[4 + f], 0.0)
                h_sum = h_sum + w * (h_around[f] - h)
                m_sum = m_sum + w * (m_around[f] - m)
            wet = code > kf
            h_sum = jnp.where(wet, h_sum, 0.0)
            t1_v[k] = h_sum
            u_v[k] = m_sum
            profile = COUPLING * (1.0 - kf / levels)
            plain = plain + jnp.where(wet, profile * m_sum, 0.0)
            scaled = scaled + jnp.where(
                wet,
                profile * (kf + 0.5) / levels * (1.0 + 2.0 * EOS_QUAD * h_sum),
                0.0,
            )
        return plain, scaled

    plain, scaled = lax.fori_loop(0, levels // STEP, diffuse_body, (zero, zero))
    mine_c[0] = plain
    mine_c[1] = scaled
    start(halo_c)

    shared(slots_1, recv_g, 1)
    coef = coefficients(totals(slots_1))
    surface_w = combined(coef, basis_1)
    back_one = combined([pltpu.roll(c, half, 1) for c in coef], basis_2)
    back_press_w = pressed_wide(back_one)

    surface_next = own(surface_w)
    back_press = own(back_press_w)

    def reverse_body(block, packed):
        for i in range(STEP):
            k = block * STEP + i
            kf = level_of(k)
            wet = code > kf
            second = t1_v[k] + jnp.where(
                wet, COUPLING * (1.0 - kf / levels) * surface_next, 0.0
            )
            masked = jnp.where(
                wet,
                u_v[k]
                + (kf + 0.5) / levels * (1.0 + 2.0 * EOS_QUAD * second) * back_press,
                0.0,
            )
            t1_v[k] = second
            m1_v[k] = masked
            packed = pack_level(k, second, masked, packed, row_2n, row_2s)
        return packed

    pack_2[...] = lax.fori_loop(0, levels // STEP, reverse_body, zero)
    start(cols_2)

    arrive(halo_c)
    total_zero = (
        back_one
        + wide(mine_c, ew_c, d_c, 0)
        + back_press_w * (wide(mine_c, ew_c, d_c, 1) + both * surface_w)
    )
    basis_3, sums_3 = basis(total_zero)
    vec_2[...] = gathered(sums_3, list(range(ENTRIES)))
    share(vec_2, slots_2, 2)

    arrive(cols_2)
    w2[13] = mixed(rp_2)

    def gradient_level(k, total):
        kf = level_of(k)
        h, m0, t, m1 = heat_v[k], m0_v[k], t1_v[k], m1_v[k]
        shift = 127 - 2 * k
        far = shift - 2 * levels
        h_around = around_of(h, w2[12], shift, rr_1, k)
        m0_around = around_of(m0, w2[12], far, rr_1, k + levels)
        t_around = around_of(t, w2[13], shift, rr_2, k)
        m1_around = around_of(m1, w2[13], far, rr_2, k + levels)
        spread = m1
        for f in range(4):
            wet = w2[f] > kf
            step = m1_around[f] - m1
            spread = spread + jnp.where(wet, w2[4 + f], 0.0) * step
            total = total + jnp.where(
                wet, (h_around[f] - h) * step + (t_around[f] - t) * (m0_around[f] - m0), 0.0
            )
        u_v[k] = spread
        return total

    def gradient_body(block, total):
        for i in range(STEP):
            total = gradient_level(block * STEP + i, total)
        return total

    diff_ref[...] = -0.5 * lax.fori_loop(0, levels // STEP, gradient_body, zero)

    shared(slots_2, recv_g, 2)
    surface = combined(coefficients(totals(slots_2)), basis_3)
    surface_ref[...] = own(surface)
    last_press = pressed(surface)

    def final_body(block, carry):
        for i in range(STEP):
            k = block * STEP + i
            kf = level_of(k)
            out_ref[k] = u_v[k] + jnp.where(
                code > kf,
                (kf + 0.5) / levels * (1.0 + 2.0 * EOS_QUAD * heat_v[k]) * last_press,
                0.0,
            )
        return carry

    lax.fori_loop(0, levels // STEP, final_body, 0)

    for copies in (halo_a, halo_b, halo_c, cols_1, cols_2):
        sent(copies)
    for turn, slots in enumerate((slots_0, slots_1, slots_2)):
        shared(slots, send_g, turn)


def shards(group, *args):
    heat, height = args[0], args[1]
    levels, rows, lanes = heat.shape
    f32 = jnp.float32
    cube = pltpu.VMEM((levels, rows, lanes), f32)
    plane = pltpu.VMEM((rows, lanes), f32)

    def halos(fields):
        return [
            pltpu.VMEM((fields, rows, lanes), f32),
            pltpu.VMEM((2, fields, rows, lanes), f32),
            pltpu.VMEM((6, fields, RIM, lanes), f32),
        ]

    columns = [
        pltpu.VMEM((rows, lanes), f32),
        pltpu.VMEM((2, rows, lanes), f32),
        pltpu.VMEM((2 * levels, lanes), f32),
        pltpu.VMEM((2 * levels, lanes), f32),
        pltpu.VMEM((2, 2 * levels, lanes), f32),
    ]
    sums = [pltpu.VMEM((1, lanes), f32), pltpu.VMEM((group, 1, lanes), f32)]
    vmem = pl.BlockSpec(memory_space=pltpu.VMEM)
    hbm = pl.BlockSpec(memory_space=pltpu.HBM)
    return pl.pallas_call(
        kernel,
        out_shape=(
            jax.ShapeDtypeStruct(heat.shape, f32),
            jax.ShapeDtypeStruct(height.shape, f32),
            jax.ShapeDtypeStruct(height.shape, f32),
        ),
        in_specs=[hbm] * 7,
        out_specs=(vmem, vmem, vmem),
        scratch_shapes=[plane] * 3
        + [pltpu.VMEM((rows, lanes), jnp.int32)] * 2
        + [cube] * 6
        + [pltpu.VMEM((14, rows, lanes), f32)]
        + halos(3)
        + halos(2)
        + halos(2)
        + columns
        + columns
        + sums * 3
        + [
            pltpu.SemaphoreType.DMA((5 + 2 * CHUNKS,)),
            pltpu.SemaphoreType.DMA((24,)),
            pltpu.SemaphoreType.DMA((24,)),
            pltpu.SemaphoreType.DMA((8,)),
            pltpu.SemaphoreType.DMA((8,)),
            pltpu.SemaphoreType.DMA((3,)),
            pltpu.SemaphoreType.DMA((3,)),
        ],
        compiler_params=pltpu.CompilerParams(
            collective_id=0, has_side_effects=True, vmem_limit_bytes=58 * 1024 * 1024
        ),
    )(*args)


def solution(mesh):
    group = mesh.shape["lon"] * mesh.shape["lat"]
    cube = P(None, ("member", "lat"), "lon")
    plane = P(("member", "lat"), "lon")
    fixed = P("lat", "lon")
    return jax.shard_map(
        functools.partial(shards, group),
        mesh=mesh,
        in_specs=(cube, plane, cube, plane, fixed, fixed, fixed),
        out_specs=(cube, plane, plane),
        check_vma=False,
    )
```
